32 devices in a mesh: ctx: 16 (over z, y, core), tp: 2 (over x).
Axes of the slice: x: 2, y: 2, z: 4, core: 2. Of those that a mesh axis runs over, the one named last changes fastest.
Arguments:
- tokens: bfloat16 [1024, 8192], P('tp', 'ctx'), may hold values from -6 to 6
- w_in: bfloat16 [8192, 24576], P('tp', 'ctx'), may hold values from -0.0625 to 0.0625
- short_taps: float32 [3, 24576], P(None, ('ctx', 'tp')), may hold values from -1 to 1
- li_residue: float32 [8192, 16], P(('ctx', 'tp')), may hold values from -0.5 to 0.5
- li_rate: float32 [8192, 16], P(('ctx', 'tp')), may hold values from 0.00048828125 to 0.1
- cotangent: bfloat16 [8192, 1024], P(('ctx', 'tp')), may hold values from -6 to 6
Outputs:
- mixed: bfloat16 [8192, 1024], P(('ctx', 'tp'))
- grad_tokens: bfloat16 [8192, 1024], P('ctx', 'tp')
The draws below stay inside these ranges and needn't reach their ends.
All inputs are finite; a program needn't handle non-finite values.
Results may differ from the reference program's by a relative error of at most 0.014.
Values may be sent and summed in bfloat16 or wider, within the bound.
A program may use at most 192 MiB of HBM per device.

```python
import math
import jax
import jax.numpy as jnp
from jax import lax

D = 8192
MODES = 16
STAPS = 3
TOKENS = 1024
CB = 256
N_CTX = 16
N_TP = 2


def shard_levels(own_key, dims, cuts, smallest, top_value):
    def one(dim, shards_of):
        steps = jax.random.uniform(jax.random.fold_in(jax.random.fold_in(own_key, 6), dim), (shards_of,), jnp.float32, smallest / len(cuts), top_value / len(cuts))
        return jnp.repeat(jnp.exp(steps), dims[dim] // shards_of).reshape((-1,) + (1,) * (len(dims) - dim - 1))

    factor_of = one(*cuts[0])
    for cut in cuts[1:]:
        factor_of = factor_of * one(*cut)
    return factor_of


def scatter_about(key, dims, deviation, reach, pieces=(), kind=jnp.bfloat16):
    factor_of = shard_levels(key, dims, pieces, -0.22, 0.18) if pieces else 1.0
    values = jax.random.normal(key, dims, jnp.float32) * deviation * factor_of
    return jnp.minimum(jnp.maximum(values, -reach), reach).astype(kind)


def setup_inputs(seed: int = 0) -> dict:
    keys = jax.random.split(jax.random.key(seed), 7)
    return {
        "tokens": scatter_about(keys[0], (TOKENS, D), 1.0, 6.0, ((0, 2), (1, 16))),
        "w_in": scatter_about(keys[1], (D, 3 * D), D ** -0.5, 0.0625, ((0, 2), (1, 16))),
        "short_taps": jnp.clip(jax.random.uniform(keys[2], (STAPS, 3 * D), jnp.float32, -1.0, 1.0) * shard_levels(keys[2], (STAPS, 3 * D), ((1, 32),), -0.4, 0.0), -1.0, 1.0),
        "li_residue": scatter_about(keys[3], (D, MODES), (4.0 / (MODES * TOKENS) ** 0.5), 0.5, ((0, 32),), jnp.float32),
        "li_rate": jnp.clip(jnp.exp(math.log(0.1) - 5.322034 * jax.random.uniform(keys[4], (D, MODES), jnp.float32) ** shard_levels(keys[4], (D, MODES), ((0, 32),), -0.2, 0.2)), 0.00048828125, 0.1),
        "cotangent": scatter_about(keys[5], (D, TOKENS), 1.0, 6.0, ((0, 32),)),
    }


HIGH = lax.Precision.HIGHEST

def mix_block(signal, taps, residue, decay):
    seq_len = signal.shape[0]
    chan_count = residue.shape[0]
    features = taps[0] * signal
    for delay in range(1, STAPS):
        padded = jnp.pad(signal, ((delay, 0), (0, 0)))[:seq_len]
        features = features + taps[delay] * padded
    features = features.reshape(seq_len, chan_count, 3)
    query_part = features[:, :, 0].T
    key_part = features[:, :, 1].T
    value_part = features[:, :, 2].T
    offsets = jnp.arange(seq_len, dtype=jnp.float32)
    kernel = jnp.einsum('cm,cml->cl', residue, jnp.exp(-decay[:, :, None] * offsets[None, None, :]), precision=HIGH)
    fft_len = 2 * seq_len
    spectrum = jnp.fft.rfft(key_part * value_part, n=fft_len, axis=1) * jnp.fft.rfft(kernel, n=fft_len, axis=1)
    filtered = jnp.fft.irfft(spectrum, n=fft_len, axis=1)[:, :seq_len]
    return query_part * filtered

def reference(tokens, w_in, short_taps, li_residue, li_rate, cotangent):
    group_count = N_CTX * N_TP
    group_cols = 3 * CB
    projected = jnp.dot(tokens, w_in, preferred_element_type=jnp.float32).astype(jnp.bfloat16)
    projected = lax.optimization_barrier(projected).astype(jnp.float32)
    signal = projected.reshape(TOKENS, group_count, group_cols).transpose(1, 0, 2)
    taps = short_taps.reshape(STAPS, group_count, group_cols).transpose(1, 0, 2)
    residue = li_residue.reshape(group_count, CB, MODES)
    decay = li_rate.reshape(group_count, CB, MODES)
    grads = cotangent.astype(jnp.float32).reshape(group_count, CB, TOKENS)

    def per_block(inputs_one):
        sig_one, tap_one, res_one, dec_one, grad_one = inputs_one
        output, pullback = jax.vjp(lambda given: mix_block(given, tap_one, res_one, dec_one), sig_one)
        return (output, pullback(grad_one)[0])
    mixed_out, grad_signal = lax.map(per_block, (signal, taps, residue, decay, grads))
    mixed_out = mixed_out.reshape(D, TOKENS).astype(jnp.bfloat16)
    grad_proj = grad_signal.astype(jnp.bfloat16).transpose(1, 0, 2).reshape(TOKENS, 3 * D)
    col_width = 3 * D // N_CTX

    def accumulate(running, block_id):
        offset = (block_id * col_width).astype(jnp.int32)
        weight_cols = lax.dynamic_slice_in_dim(w_in, offset, col_width, 1)
        grad_cols = lax.dynamic_slice_in_dim(grad_proj, offset, col_width, 1)
        partial_sum = lax.dot_general(weight_cols, grad_cols, (((1,), (1,)), ((), ())), preferred_element_type=jnp.float32)
        partial_sum = lax.optimization_barrier(partial_sum.astype(jnp.bfloat16))
        return (running + partial_sum.astype(jnp.float32), None)
    running, _ = lax.scan(accumulate, jnp.zeros((D, TOKENS), jnp.float32), jnp.arange(N_CTX, dtype=jnp.int32))
    return (mixed_out, running.astype(jnp.bfloat16))
```

```python
import functools
import math

import jax
import jax.numpy as jnp
from jax import lax
from jax.experimental import pallas as pl
from jax.experimental.pallas import tpu as pltpu
from jax.sharding import PartitionSpec as P

HIGH = lax.Precision.HIGHEST
LANES = 128


def causal_taps(signal, taps):
    seq_len = signal.shape[0]
    features = signal * taps[0]
    for delay in range(1, taps.shape[0]):
        shifted = jnp.concatenate(
            [jnp.zeros((delay, signal.shape[1]), signal.dtype), signal[: seq_len - delay]], axis=0
        )
        features = features + shifted * taps[delay]
    return features


def long_filter(signal, residue, decay):
    chan_count, seq_len = signal.shape
    tile_size = math.gcd(seq_len, 128)
    tile_count = seq_len // tile_size
    tiled = signal.reshape(chan_count, tile_count, tile_size)
    offsets = jnp.arange(tile_size, dtype=jnp.float32)
    head_taps = jnp.einsum(
        "cm,cml->cl", residue, jnp.exp(-decay[:, :, None] * offsets[None, None, :]), precision=HIGH
    )
    distance = jnp.arange(tile_size)[:, None] - jnp.arange(tile_size)[None, :]
    clipped = jnp.maximum(distance, 0)
    current = jnp.where(distance >= 0, head_taps[:, clipped], 0.0)
    inside = jnp.einsum("cts,cbs->cbt", current, tiled, precision=HIGH)
    end_decay = jnp.exp(-decay[:, :, None] * (tile_size - 1.0 - offsets)[None, None, :])
    states = jnp.einsum("cbt,cmt->cmb", tiled, end_decay, precision=HIGH)
    tile_index = jnp.arange(tile_count)
    tile_gap = tile_index[:, None] - 1 - tile_index[None, :]
    spans = (tile_size * jnp.maximum(tile_gap, 0)).astype(jnp.float32)
    carry_weight = jnp.where(tile_gap >= 0, jnp.exp(-decay[:, :, None, None] * spans), 0.0)
    carried = jnp.einsum("cmbk,cmk->cmb", carry_weight, states, precision=HIGH)
    start_decay = jnp.exp(-decay[:, :, None] * (offsets + 1.0)[None, None, :])
    across = jnp.einsum("cm,cmb,cmt->cbt", residue, carried, start_decay, precision=HIGH)
    return (inside + across).reshape(chan_count, seq_len)


def mixer(signal, taps, residue, decay):
    seq_len = signal.shape[0]
    chan_count = residue.shape[0]
    features = causal_taps(signal, taps).reshape(seq_len, chan_count, 3)
    query_part = features[:, :, 0].T
    key_part = features[:, :, 1].T
    value_part = features[:, :, 2].T
    return query_part * long_filter(key_part * value_part, residue, decay)


def shards(tokens, w_in, short_taps, li_residue, li_rate, cotangent):
    features = lax.all_gather(tokens, "ctx", axis=1, tiled=True)
    weights = lax.all_gather(w_in, "tp", axis=0, tiled=True)
    projected = jnp.dot(features, weights, preferred_element_type=jnp.float32)
    rounded = projected.astype(jnp.bfloat16)
    channels = lax.all_to_all(rounded, "tp", split_axis=1, concat_axis=0, tiled=True)
    signal = channels.astype(jnp.float32)

    def local_mix(given):
        return mixer(given, short_taps, li_residue, li_rate)

    mixed_out, pullback = jax.vjp(local_mix, signal)
    grad_signal = pullback(cotangent.astype(jnp.float32))[0]
    grad_rounded = grad_signal.astype(jnp.bfloat16)
    grad_rows = lax.all_to_all(grad_rounded, "tp", split_axis=0, concat_axis=1, tiled=True)
    summed = lax.psum_scatter(
        lax.dot_general(
            weights, grad_rows, (((1,), (1,)), ((), ())), preferred_element_type=jnp.float32
        ).astype(jnp.bfloat16),
        "ctx",
        scatter_dimension=0,
        tiled=True,
    )
    return (mixed_out.astype(jnp.bfloat16), summed)


def swap_pairs(n_ctx, n_tp):
    half = n_ctx // n_tp
    pairs = []
    for ctx in range(n_ctx):
        for tp in range(n_tp):
            owner = (tp * half + ctx % half) * n_tp + ctx // half
            pairs.append((owner, ctx * n_tp + tp))
    return pairs


def mix_kernel(seq_len, chans, modes, chunks, proj_ref, spread_ref, taps_ref, rate_ref, res_ref,
               cot_ref, mixed_ref, grad_ref, planes, feats, sums, grads, outs, backs, rates, powers):
    halves = chans // LANES
    rows = chunks * halves
    steps = seq_len // chunks
    tile = steps

    def multiply(i, carry):
        at = pl.ds(pl.multiple_of(i * tile, tile), tile)
        planes[at, :] = jnp.dot(proj_ref[at, :], spread_ref[...], preferred_element_type=jnp.float32)
        return carry

    lax.fori_loop(0, chunks, multiply, 0)

    row_id = lax.broadcasted_iota(jnp.int32, (seq_len, LANES), 0)
    taps_count = taps_ref.shape[0]
    for col in range(3 * halves):
        lanes = slice(col * LANES, (col + 1) * LANES)
        plane = planes[:, lanes]
        total = plane * taps_ref[0:1, lanes]
        for delay in range(1, taps_count):
            shifted = jnp.where(row_id >= delay, pltpu.roll(plane, delay, 0), 0.0)
            total = total + shifted * taps_ref[delay:delay + 1, lanes]
        feats[:, lanes] = total

    for half in range(halves):
        lanes = [slice((r * halves + half) * LANES, (r * halves + half + 1) * LANES) for r in range(3)]
        for chunk in range(chunks):
            at = slice(chunk * steps, (chunk + 1) * steps)
            row = pl.ds(chunk * halves + half, steps, stride=rows)
            sums[row, :] = feats[at, lanes[1]] * feats[at, lanes[2]]
            cot = cot_ref[half * LANES:(half + 1) * LANES, at].astype(jnp.float32).T
            planes[at, half * LANES:(half + 1) * LANES] = cot
            grads[row, :] = cot * feats[at, lanes[0]]

    chunk_id = lax.broadcasted_iota(jnp.int32, (rows, LANES), 0) // halves
    for m in range(modes):
        rates[m] = jnp.exp(-rate_ref[m])
        powers[m] = jnp.exp(-rate_ref[m] * float(steps))

    def scan(source, result, backward):
        def place(step):
            at = steps - 1 - step if backward else step
            return pl.ds(pl.multiple_of(at * rows, rows), rows)

        def ends(step, states):
            u = source[place(step), :]
            return tuple(rates[m] * states[m] + u for m in range(modes))

        zeros = tuple(jnp.zeros((rows, LANES), jnp.float32) for _ in range(modes))
        last = lax.fori_loop(0, steps, ends, zeros, unroll=4)
        first = []
        for m in range(modes):
            carry = jnp.zeros((rows, LANES), jnp.float32)
            for _ in range(chunks - 1):
                total = powers[m] * carry + last[m]
                if backward:
                    carry = jnp.where(chunk_id < chunks - 1, pltpu.roll(total, rows - halves, 0), 0.0)
                else:
                    carry = jnp.where(chunk_id > 0, pltpu.roll(total, halves, 0), 0.0)
            first.append(carry)

        def run(step, states):
            u = source[place(step), :]
            states = tuple(rates[m] * states[m] + u for m in range(modes))
            terms = [res_ref[m] * states[m] for m in range(modes)]
            while len(terms) > 1:
                terms = [a + b for a, b in zip(terms[0::2], terms[1::2])]
            result[place(step), :] = terms[0]
            return states

        lax.fori_loop(0, steps, run, tuple(first), unroll=4)

    scan(sums, outs, False)
    scan(grads, backs, True)

    for half in range(halves):
        lanes = [slice((r * halves + half) * LANES, (r * halves + half + 1) * LANES) for r in range(3)]
        for chunk in range(chunks):
            at = slice(chunk * steps, (chunk + 1) * steps)
            row = pl.ds(chunk * halves + half, steps, stride=rows)
            y = outs[row, :]
            du = backs[row, :]
            mixed_ref[half * LANES:(half + 1) * LANES, at] = (feats[at, lanes[0]] * y).T.astype(jnp.bfloat16)
            cot = planes[at, half * LANES:(half + 1) * LANES]
            key = feats[at, lanes[1]]
            feats[at, lanes[0]] = cot * y
            feats[at, lanes[1]] = du * feats[at, lanes[2]]
            feats[at, lanes[2]] = du * key

    for col in range(3 * halves):
        lanes = slice(col * LANES, (col + 1) * LANES)
        grad = feats[:, lanes]
        total = grad * taps_ref[0:1, lanes]
        for delay in range(1, taps_count):
            shifted = jnp.where(row_id < seq_len - delay, pltpu.roll(grad, seq_len - delay, 0), 0.0)
            total = total + shifted * taps_ref[delay:delay + 1, lanes]
        planes[:, lanes] = total

    def gather(i, carry):
        at = pl.ds(pl.multiple_of(i * tile, tile), tile)
        grad_ref[at, :] = lax.dot_general(
            planes[at, :].astype(jnp.bfloat16), spread_ref[...], (((1,), (1,)), ((), ())),
            preferred_element_type=jnp.float32,
        ).astype(jnp.bfloat16)
        return carry

    lax.fori_loop(0, chunks, gather, 0)


def mix(projected, short_taps, li_residue, li_rate, cotangent):
    seq_len, cols = projected.shape
    chans, modes = li_rate.shape
    halves = chans // LANES
    rows = 8
    chunks = rows // halves
    source = jnp.arange(cols)[:, None]
    target = jnp.arange(cols)[None, :]
    spread = (source == 3 * (target % chans) + target // chans).astype(jnp.bfloat16)
    taps = short_taps.reshape(-1, chans, 3).transpose(0, 2, 1).reshape(-1, cols)

    def per_row(values):
        return jnp.tile(values.T.reshape(modes, halves, LANES), (1, chunks, 1))

    f32 = functools.partial(pltpu.VMEM, dtype=jnp.float32)
    vmem = pl.BlockSpec(memory_space=pltpu.VMEM)
    return pl.pallas_call(
        functools.partial(mix_kernel, seq_len, chans, modes, chunks),
        out_shape=(
            jax.ShapeDtypeStruct((chans, seq_len), jnp.bfloat16),
            jax.ShapeDtypeStruct((seq_len, cols), jnp.bfloat16),
        ),
        in_specs=[vmem] * 6,
        out_specs=(vmem, vmem),
        scratch_shapes=[
            f32((seq_len, cols)),
            f32((seq_len, cols)),
            f32((seq_len * halves, LANES)),
            f32((seq_len * halves, LANES)),
            f32((seq_len * halves, LANES)),
            f32((seq_len * halves, LANES)),
            f32((modes, rows, LANES)),
            f32((modes, rows, LANES)),
        ],
        compiler_params=pltpu.CompilerParams(vmem_limit_bytes=40 * 1024 * 1024),
        cost_estimate=pl.CostEstimate(
            flops=20 * 10**9, bytes_accessed=6 * seq_len * cols, transcendentals=0
        ),
        name="mix",
    )(projected, spread, taps, per_row(li_rate), per_row(li_residue), cotangent)


def fast_shards(n_ctx, n_tp, tokens, w_in, short_taps, li_residue, li_rate, cotangent):
    pairs = swap_pairs(n_ctx, n_tp)
    tp = lax.axis_index("tp")
    rows, cols = w_in.shape
    half_cols = cols // 2
    piece = lax.ppermute(tokens, ("ctx", "tp"), pairs)
    features = lax.all_gather(piece, "ctx", axis=1, tiled=True)

    def partial(side):
        weights = lax.dynamic_slice_in_dim(w_in, side * half_cols, half_cols, 1)
        return jnp.concatenate(
            [
                jnp.dot(features[:, i * rows:(i + 1) * rows], weights, preferred_element_type=jnp.float32)
                for i in range(n_tp)
            ],
            axis=0,
        )

    other = lax.ppermute(partial(1 - tp).astype(jnp.bfloat16), "tp", [(0, 1), (1, 0)])
    projected = (partial(tp) + other.astype(jnp.float32)).astype(jnp.bfloat16)
    mixed, grad = mix(projected, short_taps, li_residue, li_rate, cotangent)
    grad_cols = lax.all_gather(grad, "tp", axis=1, tiled=True)
    count = tokens.shape[0]
    products = jnp.concatenate(
        [
            lax.dot_general(
                w_in, grad_cols[i * count:(i + 1) * count], (((1,), (1,)), ((), ())),
                preferred_element_type=jnp.float32,
            ).astype(jnp.bfloat16)
            for i in range(n_tp)
        ],
        axis=0,
    )
    summed = lax.psum_scatter(products, "ctx", scatter_dimension=0, tiled=True)
    back = [(b, a) for a, b in pairs]
    return mixed, lax.ppermute(summed, ("ctx", "tp"), back)


def solution(mesh):
    n_ctx, n_tp = mesh.shape["ctx"], mesh.shape["tp"]
    body = functools.partial(fast_shards, n_ctx, n_tp) if (n_ctx, n_tp) == (16, 2) else shards
    in_specs = (
        P("tp", "ctx"),
        P("tp", "ctx"),
        P(None, ("ctx", "tp")),
        P(("ctx", "tp"), None),
        P(("ctx", "tp"), None),
        P(("ctx", "tp"), None),
    )
    out_specs = (P(("ctx", "tp"), None), P("ctx", "tp"))
    return jax.shard_map(body, mesh=mesh, in_specs=in_specs, out_specs=out_specs, check_vma=False)
```

```python
import functools
import math

import jax
import jax.numpy as jnp
from jax import lax
from jax.experimental import pallas as pl
from jax.experimental.pallas import tpu as pltpu
from jax.sharding import PartitionSpec as P

HIGH = lax.Precision.HIGHEST
LANES = 128


def causal_taps(signal, taps):
    seq_len = signal.shape[0]
    features = signal * taps[0]
    for delay in range(1, taps.shape[0]):
        shifted = jnp.concatenate(
            [jnp.zeros((delay, signal.shape[1]), signal.dtype), signal[: seq_len - delay]], axis=0
        )
        features = features + shifted * taps[delay]
    return features


def long_filter(signal, residue, decay):
    chan_count, seq_len = signal.shape
    tile_size = math.gcd(seq_len, 128)
    tile_count = seq_len // tile_size
    tiled = signal.reshape(chan_count, tile_count, tile_size)
    offsets = jnp.arange(tile_size, dtype=jnp.float32)
    head_taps = jnp.einsum(
        "cm,cml->cl", residue, jnp.exp(-decay[:, :, None] * offsets[None, None, :]), precision=HIGH
    )
    distance = jnp.arange(tile_size)[:, None] - jnp.arange(tile_size)[None, :]
    clipped = jnp.maximum(distance, 0)
    current = jnp.where(distance >= 0, head_taps[:, clipped], 0.0)
    inside = jnp.einsum("cts,cbs->cbt", current, tiled, precision=HIGH)
    end_decay = jnp.exp(-decay[:, :, None] * (tile_size - 1.0 - offsets)[None, None, :])
    states = jnp.einsum("cbt,cmt->cmb", tiled, end_decay, precision=HIGH)
    tile_index = jnp.arange(tile_count)
    tile_gap = tile_index[:, None] - 1 - tile_index[None, :]
    spans = (tile_size * jnp.maximum(tile_gap, 0)).astype(jnp.float32)
    carry_weight = jnp.where(tile_gap >= 0, jnp.exp(-decay[:, :, None, None] * spans), 0.0)
    carried = jnp.einsum("cmbk,cmk->cmb", carry_weight, states, precision=HIGH)
    start_decay = jnp.exp(-decay[:, :, None] * (offsets + 1.0)[None, None, :])
    across = jnp.einsum("cm,cmb,cmt->cbt", residue, carried, start_decay, precision=HIGH)
    return (inside + across).reshape(chan_count, seq_len)


def mixer(signal, taps, residue, decay):
    seq_len = signal.shape[0]
    chan_count = residue.shape[0]
    features = causal_taps(signal, taps).reshape(seq_len, chan_count, 3)
    query_part = features[:, :, 0].T
    key_part = features[:, :, 1].T
    value_part = features[:, :, 2].T
    return query_part * long_filter(key_part * value_part, residue, decay)


def shards(tokens, w_in, short_taps, li_residue, li_rate, cotangent):
    features = lax.all_gather(tokens, "ctx", axis=1, tiled=True)
    weights = lax.all_gather(w_in, "tp", axis=0, tiled=True)
    projected = jnp.dot(features, weights, preferred_element_type=jnp.float32)
    rounded = projected.astype(jnp.bfloat16)
    channels = lax.all_to_all(rounded, "tp", split_axis=1, concat_axis=0, tiled=True)
    signal = channels.astype(jnp.float32)

    def local_mix(given):
        return mixer(given, short_taps, li_residue, li_rate)

    mixed_out, pullback = jax.vjp(local_mix, signal)
    grad_signal = pullback(cotangent.astype(jnp.float32))[0]
    grad_rounded = grad_signal.astype(jnp.bfloat16)
    grad_rows = lax.all_to_all(grad_rounded, "tp", split_axis=0, concat_axis=1, tiled=True)
    summed = lax.psum_scatter(
        lax.dot_general(
            weights, grad_rows, (((1,), (1,)), ((), ())), preferred_element_type=jnp.float32
        ).astype(jnp.bfloat16),
        "ctx",
        scatter_dimension=0,
        tiled=True,
    )
    return (mixed_out.astype(jnp.bfloat16), summed)


MESH = pl.DeviceIdType.MESH
TURNS = (4, 3, -3, 2, -2, 1, -1, 0)


def ring_place(ctx):
    z, y = ctx // 4, (ctx // 2) % 2
    return z + y * (7 - 2 * z)


def ring_ctx(place, core):
    y = place // 4
    z = place + y * (7 - 2 * place)
    return z * 4 + y * 2 + core


def greet(others, partner, ctx, tp):
    barrier = pltpu.get_barrier_semaphore()
    for other in others:
        pl.semaphore_signal(barrier, inc=1, device_id=other, device_id_type=MESH)

    @pl.when(ctx // 8 != tp)
    def _():
        pl.semaphore_signal(barrier, inc=1, device_id=partner, device_id_type=MESH)
        pl.semaphore_wait(barrier, len(others) + 1)

    @pl.when(ctx // 8 == tp)
    def _():
        pl.semaphore_wait(barrier, len(others))


def scatter_kernel(grad_ref, w_hbm, out_ref, w_ref, cols, own, core_send, core_recv, right_send, right_recv,
                   left_send, left_recv, last, landed, local_sem, x_ssem, x_rsem, core_ssem, core_rsem,
                   r_ssem, r_rsem, l_ssem, l_rsem, end_ssem, end_rsem):
    ctx, tp = lax.axis_index("ctx"), lax.axis_index("tp")
    core, place = ctx % 2, ring_place(ctx)
    across = (ctx, 1 - tp)
    beside = (ctx + 1 - 2 * core, tp)
    right = (ring_ctx((place + 1) % 8, core), tp)
    left = (ring_ctx((place + 7) % 8, core), tp)
    owner = (tp * 8 + ctx % 8, ctx // 8)
    count, width = own.shape[2], grad_ref.shape[1]
    load = pltpu.make_async_copy(w_hbm, w_ref, local_sem.at[0])
    load.start()
    keep = pltpu.make_async_copy(grad_ref, cols.at[tp], local_sem.at[1])
    keep.start()
    greet([across, beside, right, left], owner, ctx, tp)

    def send(src, dst, ssem, rsem, where):
        copy = pltpu.make_async_remote_copy(
            src_ref=src, dst_ref=dst, send_sem=ssem, recv_sem=rsem, device_id=where, device_id_type=MESH
        )
        copy.start()
        return copy

    near = ctx // 8
    shares = []
    for turn, half in enumerate((1 - near, near)):
        at = pl.ds(pl.multiple_of(half * count, count), count)
        shares.append(send(grad_ref.at[at], cols.at[tp, at], x_ssem.at[turn], x_rsem.at[turn], across))
    load.wait()
    keep.wait()

    def product(piece, dst):
        row = (piece % 8) * count
        token = pl.ds(pl.multiple_of((piece // 8) * count, count), count)

        def tile(i, carry):
            at = pl.ds(pl.multiple_of(row + i * 256, 256), 256)
            total = None
            for side in range(2):
                term = lax.dot_general(
                    w_ref[at, side * width:(side + 1) * width], cols[side, token, :],
                    (((1,), (1,)), ((), ())), preferred_element_type=jnp.float32,
                )
                total = term if total is None else total + term
            dst[pl.ds(pl.multiple_of(i * 256, 256), 256), :] = total.astype(dst.dtype)
            return carry

        lax.fori_loop(0, count // 256, tile, 0)

    to_core = [None] * 8

    def both(k):
        target = (place + TURNS[k] + 8) % 8
        product(ring_ctx(target, 1 - core), core_send.at[k])
        to_core[k] = send(core_send.at[k], core_recv.at[k], core_ssem.at[k], core_rsem.at[k], beside)
        product(ring_ctx(target, core), own.at[k])

    def mine(k, rows):
        return own[k, rows, :] + core_recv[k, rows, :].astype(jnp.float32)

    top, bottom, whole = slice(0, count // 2), slice(count // 2, count), slice(0, count)
    shares[0].wait_recv()
    both(0)
    shares[1].wait_recv()
    to_core[0].wait_recv()
    right_send[0, top, :] = mine(0, top).astype(jnp.bfloat16)
    left_send[0, bottom, :] = mine(0, bottom).astype(jnp.bfloat16)
    to_right = [send(right_send.at[0, top], right_recv.at[0, top], r_ssem.at[0], r_rsem.at[0], right)]
    to_left = [send(left_send.at[0, bottom], left_recv.at[0, bottom], l_ssem.at[0], l_rsem.at[0], left)]
    for k in (1, 2, 3, 4):
        both(k)
    for step in (1, 2, 3):
        k = 2 * step - 1
        to_core[k].wait_recv()
        to_right[step - 1].wait_recv()
        if step == 1:
            right_send[1, top, :] = (mine(k, top) + right_recv[0, top, :].astype(jnp.float32)).astype(jnp.bfloat16)
            right_send[1, bottom, :] = mine(k, bottom).astype(jnp.bfloat16)
        else:
            right_send[step] = (mine(k, whole) + right_recv[step - 1].astype(jnp.float32)).astype(jnp.bfloat16)
        to_right.append(send(right_send.at[step], right_recv.at[step], r_ssem.at[step], r_rsem.at[step], right))
        k += 1
        to_core[k].wait_recv()
        to_left[step - 1].wait_recv()
        if step == 1:
            left_send[1, top, :] = mine(k, top).astype(jnp.bfloat16)
            left_send[1, bottom, :] = (mine(k, bottom) + left_recv[0, bottom, :].astype(jnp.float32)).astype(jnp.bfloat16)
        else:
            left_send[step] = (mine(k, whole) + left_recv[step - 1].astype(jnp.float32)).astype(jnp.bfloat16)
        to_left.append(send(left_send.at[step], left_recv.at[step], l_ssem.at[step], l_rsem.at[step], left))
        if step == 1:
            for k in (5, 6, 7):
                both(k)
    to_core[7].wait_recv()
    to_right[3].wait_recv()
    to_left[3].wait_recv()
    total = mine(7, whole) + right_recv[3].astype(jnp.float32) + left_recv[3].astype(jnp.float32)
    last[...] = total.astype(jnp.bfloat16)

    @pl.when(near != tp)
    def _():
        end = send(last, landed, end_ssem, end_rsem, owner)
        end.wait()
        out_ref[...] = landed[...]

    @pl.when(near == tp)
    def _():
        out_ref[...] = last[...]

    for copy in shares + to_core + to_right + to_left:
        copy.wait_send()


def multiply_scatter(w_in, grad):
    rows, cols = w_in.shape
    seq_len, width = grad.shape
    block = rows // 8
    bf16 = functools.partial(pltpu.VMEM, dtype=jnp.bfloat16)
    dma = pltpu.SemaphoreType.DMA
    vmem = pl.BlockSpec(memory_space=pltpu.VMEM)
    return pl.pallas_call(
        scatter_kernel,
        out_shape=jax.ShapeDtypeStruct((block, block), jnp.bfloat16),
        in_specs=[vmem, pl.BlockSpec(memory_space=pl.ANY)],
        out_specs=vmem,
        scratch_shapes=[
            bf16((rows, cols)),
            bf16((2, seq_len, width)),
            pltpu.VMEM((8, block, block), jnp.float32),
            bf16((8, block, block)),
            bf16((8, block, block)),
            bf16((4, block, block)),
            bf16((4, block, block)),
            bf16((4, block, block)),
            bf16((4, block, block)),
            bf16((block, block)),
            bf16((block, block)),
            dma((2,)), dma((2,)), dma((2,)), dma((8,)), dma((8,)),
            dma((4,)), dma((4,)), dma((4,)), dma((4,)), dma, dma,
        ],
        compiler_params=pltpu.CompilerParams(
            collective_id=1, has_side_effects=True, vmem_limit_bytes=56 * 1024 * 1024
        ),
        cost_estimate=pl.CostEstimate(
            flops=2 * rows * cols * seq_len, bytes_accessed=2 * rows * cols, transcendentals=0
        ),
        name="multiply_scatter",
    )(grad, w_in)


def swap_pairs(n_ctx, n_tp):
    half = n_ctx // n_tp
    pairs = []
    for ctx in range(n_ctx):
        for tp in range(n_tp):
            owner = (tp * half + ctx % half) * n_tp + ctx // half
            pairs.append((owner, ctx * n_tp + tp))
    return pairs


def mix_kernel(seq_len, chans, modes, chunks, proj_ref, spread_ref, taps_ref, rate_ref, res_ref,
               cot_ref, mixed_ref, grad_ref, planes, feats, sums, grads, outs, backs, rates, powers):
    halves = chans // LANES
    rows = chunks * halves
    steps = seq_len // chunks
    tile = steps

    def multiply(i, carry):
        at = pl.ds(pl.multiple_of(i * tile, tile), tile)
        planes[at, :] = jnp.dot(proj_ref[at, :], spread_ref[...], preferred_element_type=jnp.float32)
        return carry

    lax.fori_loop(0, chunks, multiply, 0)

    row_id = lax.broadcasted_iota(jnp.int32, (seq_len, LANES), 0)
    taps_count = taps_ref.shape[0]
    for col in range(3 * halves):
        lanes = slice(col * LANES, (col + 1) * LANES)
        plane = planes[:, lanes]
        total = plane * taps_ref[0:1, lanes]
        for delay in range(1, taps_count):
            shifted = jnp.where(row_id >= delay, pltpu.roll(plane, delay, 0), 0.0)
            total = total + shifted * taps_ref[delay:delay + 1, lanes]
        feats[:, lanes] = total

    for half in range(halves):
        lanes = [slice((r * halves + half) * LANES, (r * halves + half + 1) * LANES) for r in range(3)]
        for chunk in range(chunks):
            at = slice(chunk * steps, (chunk + 1) * steps)
            row = pl.ds(chunk * halves + half, steps, stride=rows)
            sums[row, :] = feats[at, lanes[1]] * feats[at, lanes[2]]
            cot = cot_ref[half * LANES:(half + 1) * LANES, at].astype(jnp.float32).T
            planes[at, half * LANES:(half + 1) * LANES] = cot
            grads[row, :] = cot * feats[at, lanes[0]]

    chunk_id = lax.broadcasted_iota(jnp.int32, (rows, LANES), 0) // halves
    for m in range(modes):
        rates[m] = jnp.exp(-rate_ref[m])
        powers[m] = jnp.exp(-rate_ref[m] * float(steps))

    def scan(source, result, backward):
        def place(step):
            at = steps - 1 - step if backward else step
            return pl.ds(pl.multiple_of(at * rows, rows), rows)

        def ends(step, states):
            u = source[place(step), :]
            return tuple(rates[m] * states[m] + u for m in range(modes))

        zeros = tuple(jnp.zeros((rows, LANES), jnp.float32) for _ in range(modes))
        last = lax.fori_loop(0, steps, ends, zeros, unroll=4)
        first = []
        for m in range(modes):
            carry = jnp.zeros((rows, LANES), jnp.float32)
            for _ in range(chunks - 1):
                total = powers[m] * carry + last[m]
                if backward:
                    carry = jnp.where(chunk_id < chunks - 1, pltpu.roll(total, rows - halves, 0), 0.0)
                else:
                    carry = jnp.where(chunk_id > 0, pltpu.roll(total, halves, 0), 0.0)
            first.append(carry)

        def run(step, states):
            u = source[place(step), :]
            states = tuple(rates[m] * states[m] + u for m in range(modes))
            terms = [res_ref[m] * states[m] for m in range(modes)]
            while len(terms) > 1:
                terms = [a + b for a, b in zip(terms[0::2], terms[1::2])]
            result[place(step), :] = terms[0]
            return states

        lax.fori_loop(0, steps, run, tuple(first), unroll=4)

    scan(sums, outs, False)
    scan(grads, backs, True)

    for half in range(halves):
        lanes = [slice((r * halves + half) * LANES, (r * halves + half + 1) * LANES) for r in range(3)]
        for chunk in range(chunks):
            at = slice(chunk * steps, (chunk + 1) * steps)
            row = pl.ds(chunk * halves + half, steps, stride=rows)
            y = outs[row, :]
            du = backs[row, :]
            mixed_ref[half * LANES:(half + 1) * LANES, at] = (feats[at, lanes[0]] * y).T.astype(jnp.bfloat16)
            cot = planes[at, half * LANES:(half + 1) * LANES]
            key = feats[at, lanes[1]]
            feats[at, lanes[0]] = cot * y
            feats[at, lanes[1]] = du * feats[at, lanes[2]]
            feats[at, lanes[2]] = du * key

    for col in range(3 * halves):
        lanes = slice(col * LANES, (col + 1) * LANES)
        grad = feats[:, lanes]
        total = grad * taps_ref[0:1, lanes]
        for delay in range(1, taps_count):
            shifted = jnp.where(row_id < seq_len - delay, pltpu.roll(grad, seq_len - delay, 0), 0.0)
            total = total + shifted * taps_ref[delay:delay + 1, lanes]
        planes[:, lanes] = total

    def gather(i, carry):
        at = pl.ds(pl.multiple_of(i * tile, tile), tile)
        grad_ref[at, :] = lax.dot_general(
            planes[at, :].astype(jnp.bfloat16), spread_ref[...], (((1,), (1,)), ((), ())),
            preferred_element_type=jnp.float32,
        ).astype(jnp.bfloat16)
        return carry

    lax.fori_loop(0, chunks, gather, 0)


def mix(projected, short_taps, li_residue, li_rate, cotangent):
    seq_len, cols = projected.shape
    chans, modes = li_rate.shape
    halves = chans // LANES
    rows = 8
    chunks = rows // halves
    source = jnp.arange(cols)[:, None]
    target = jnp.arange(cols)[None, :]
    spread = (source == 3 * (target % chans) + target // chans).astype(jnp.bfloat16)
    taps = short_taps.reshape(-1, chans, 3).transpose(0, 2, 1).reshape(-1, cols)

    def per_row(values):
        return jnp.tile(values.T.reshape(modes, halves, LANES), (1, chunks, 1))

    f32 = functools.partial(pltpu.VMEM, dtype=jnp.float32)
    vmem = pl.BlockSpec(memory_space=pltpu.VMEM)
    return pl.pallas_call(
        functools.partial(mix_kernel, seq_len, chans, modes, chunks),
        out_shape=(
            jax.ShapeDtypeStruct((chans, seq_len), jnp.bfloat16),
            jax.ShapeDtypeStruct((seq_len, cols), jnp.bfloat16),
        ),
        in_specs=[vmem] * 6,
        out_specs=(vmem, vmem),
        scratch_shapes=[
            f32((seq_len, cols)),
            f32((seq_len, cols)),
            f32((seq_len * halves, LANES)),
            f32((seq_len * halves, LANES)),
            f32((seq_len * halves, LANES)),
            f32((seq_len * halves, LANES)),
            f32((modes, rows, LANES)),
            f32((modes, rows, LANES)),
        ],
        compiler_params=pltpu.CompilerParams(vmem_limit_bytes=40 * 1024 * 1024),
        cost_estimate=pl.CostEstimate(
            flops=20 * 10**9, bytes_accessed=6 * seq_len * cols, transcendentals=0
        ),
        name="mix",
    )(projected, spread, taps, per_row(li_rate), per_row(li_residue), cotangent)


def fast_shards(n_ctx, n_tp, tokens, w_in, short_taps, li_residue, li_rate, cotangent):
    pairs = swap_pairs(n_ctx, n_tp)
    tp = lax.axis_index("tp")
    rows, cols = w_in.shape
    half_cols = cols // 2
    piece = lax.ppermute(tokens, ("ctx", "tp"), pairs)
    features = lax.all_gather(piece, "ctx", axis=1, tiled=True)

    def partial(side):
        weights = lax.dynamic_slice_in_dim(w_in, side * half_cols, half_cols, 1)
        return jnp.concatenate(
            [
                jnp.dot(features[:, i * rows:(i + 1) * rows], weights, preferred_element_type=jnp.float32)
                for i in range(n_tp)
            ],
            axis=0,
        )

    other = lax.ppermute(partial(1 - tp).astype(jnp.bfloat16), "tp", [(0, 1), (1, 0)])
    projected = (partial(tp) + other.astype(jnp.float32)).astype(jnp.bfloat16)
    mixed, grad = mix(projected, short_taps, li_residue, li_rate, cotangent)
    return mixed, multiply_scatter(w_in, grad)


def solution(mesh):
    n_ctx, n_tp = mesh.shape["ctx"], mesh.shape["tp"]
    body = functools.partial(fast_shards, n_ctx, n_tp) if (n_ctx, n_tp) == (16, 2) else shards
    in_specs = (
        P("tp", "ctx"),
        P("tp", "ctx"),
        P(None, ("ctx", "tp")),
        P(("ctx", "tp"), None),
        P(("ctx", "tp"), None),
        P(("ctx", "tp"), None),
    )
    out_specs = (P(("ctx", "tp"), None), P("ctx", "tp"))
    return jax.shard_map(body, mesh=mesh, in_specs=in_specs, out_specs=out_specs, check_vma=False)
```

```python
import functools
import math

import jax
import jax.numpy as jnp
from jax import lax
from jax.experimental import pallas as pl
from jax.experimental.pallas import tpu as pltpu
from jax.sharding import PartitionSpec as P

HIGH = lax.Precision.HIGHEST
LANES = 128


def causal_taps(signal, taps):
    seq_len = signal.shape[0]
    features = signal * taps[0]
    for delay in range(1, taps.shape[0]):
        shifted = jnp.concatenate(
            [jnp.zeros((delay, signal.shape[1]), signal.dtype), signal[: seq_len - delay]], axis=0
        )
        features = features + shifted * taps[delay]
    return features


def long_filter(signal, residue, decay):
    chan_count, seq_len = signal.shape
    tile_size = math.gcd(seq_len, 128)
    tile_count = seq_len // tile_size
    tiled = signal.reshape(chan_count, tile_count, tile_size)
    offsets = jnp.arange(tile_size, dtype=jnp.float32)
    head_taps = jnp.einsum(
        "cm,cml->cl", residue, jnp.exp(-decay[:, :, None] * offsets[None, None, :]), precision=HIGH
    )
    distance = jnp.arange(tile_size)[:, None] - jnp.arange(tile_size)[None, :]
    clipped = jnp.maximum(distance, 0)
    current = jnp.where(distance >= 0, head_taps[:, clipped], 0.0)
    inside = jnp.einsum("cts,cbs->cbt", current, tiled, precision=HIGH)
    end_decay = jnp.exp(-decay[:, :, None] * (tile_size - 1.0 - offsets)[None, None, :])
    states = jnp.einsum("cbt,cmt->cmb", tiled, end_decay, precision=HIGH)
    tile_index = jnp.arange(tile_count)
    tile_gap = tile_index[:, None] - 1 - tile_index[None, :]
    spans = (tile_size * jnp.maximum(tile_gap, 0)).astype(jnp.float32)
    carry_weight = jnp.where(tile_gap >= 0, jnp.exp(-decay[:, :, None, None] * spans), 0.0)
    carried = jnp.einsum("cmbk,cmk->cmb", carry_weight, states, precision=HIGH)
    start_decay = jnp.exp(-decay[:, :, None] * (offsets + 1.0)[None, None, :])
    across = jnp.einsum("cm,cmb,cmt->cbt", residue, carried, start_decay, precision=HIGH)
    return (inside + across).reshape(chan_count, seq_len)


def mixer(signal, taps, residue, decay):
    seq_len = signal.shape[0]
    chan_count = residue.shape[0]
    features = causal_taps(signal, taps).reshape(seq_len, chan_count, 3)
    query_part = features[:, :, 0].T
    key_part = features[:, :, 1].T
    value_part = features[:, :, 2].T
    return query_part * long_filter(key_part * value_part, residue, decay)


def shards(tokens, w_in, short_taps, li_residue, li_rate, cotangent):
    features = lax.all_gather(tokens, "ctx", axis=1, tiled=True)
    weights = lax.all_gather(w_in, "tp", axis=0, tiled=True)
    projected = jnp.dot(features, weights, preferred_element_type=jnp.float32)
    rounded = projected.astype(jnp.bfloat16)
    channels = lax.all_to_all(rounded, "tp", split_axis=1, concat_axis=0, tiled=True)
    signal = channels.astype(jnp.float32)

    def local_mix(given):
        return mixer(given, short_taps, li_residue, li_rate)

    mixed_out, pullback = jax.vjp(local_mix, signal)
    grad_signal = pullback(cotangent.astype(jnp.float32))[0]
    grad_rounded = grad_signal.astype(jnp.bfloat16)
    grad_rows = lax.all_to_all(grad_rounded, "tp", split_axis=0, concat_axis=1, tiled=True)
    summed = lax.psum_scatter(
        lax.dot_general(
            weights, grad_rows, (((1,), (1,)), ((), ())), preferred_element_type=jnp.float32
        ).astype(jnp.bfloat16),
        "ctx",
        scatter_dimension=0,
        tiled=True,
    )
    return (mixed_out.astype(jnp.bfloat16), summed)


MESH = pl.DeviceIdType.MESH
TURNS = (4, 3, -3, 2, -2, 1, -1, 0)


def ring_place(ctx):
    z, y = ctx // 4, (ctx // 2) % 2
    return z + y * (7 - 2 * z)


def ring_ctx(place, core):
    y = place // 4
    z = place + y * (7 - 2 * place)
    return z * 4 + y * 2 + core


def greet(others, partner, ctx, tp):
    barrier = pltpu.get_barrier_semaphore()
    for other in others:
        pl.semaphore_signal(barrier, inc=1, device_id=other, device_id_type=MESH)

    @pl.when(ctx // 8 != tp)
    def _():
        pl.semaphore_signal(barrier, inc=1, device_id=partner, device_id_type=MESH)
        pl.semaphore_wait(barrier, len(others) + 1)

    @pl.when(ctx // 8 == tp)
    def _():
        pl.semaphore_wait(barrier, len(others))


def scatter_kernel(grad_ref, w_hbm, out_ref, w_ref, cols, own, core_send, core_recv, right_send, right_recv,
                   left_send, left_recv, last, landed, local_sem, x_ssem, x_rsem, core_ssem, core_rsem,
                   r_ssem, r_rsem, l_ssem, l_rsem, end_ssem, end_rsem):
    ctx, tp = lax.axis_index("ctx"), lax.axis_index("tp")
    core, place = ctx % 2, ring_place(ctx)
    across = (ctx, 1 - tp)
    beside = (ctx + 1 - 2 * core, tp)
    right = (ring_ctx((place + 1) % 8, core), tp)
    left = (ring_ctx((place + 7) % 8, core), tp)
    owner = (tp * 8 + ctx % 8, ctx // 8)
    count, width = own.shape[2], grad_ref.shape[1]
    load = pltpu.make_async_copy(w_hbm, w_ref, local_sem.at[0])
    load.start()
    keep = pltpu.make_async_copy(grad_ref, cols.at[tp], local_sem.at[1])
    keep.start()
    greet([across, beside, right, left], owner, ctx, tp)

    def send(src, dst, ssem, rsem, where):
        copy = pltpu.make_async_remote_copy(
            src_ref=src, dst_ref=dst, send_sem=ssem, recv_sem=rsem, device_id=where, device_id_type=MESH
        )
        copy.start()
        return copy

    near = ctx // 8
    shares = []
    for turn, half in enumerate((1 - near, near)):
        at = pl.ds(pl.multiple_of(half * count, count), count)
        shares.append(send(grad_ref.at[at], cols.at[tp, at], x_ssem.at[turn], x_rsem.at[turn], across))
    load.wait()
    keep.wait()

    def product(piece, dst):
        row = (piece % 8) * count
        token = pl.ds(pl.multiple_of((piece // 8) * count, count), count)

        def tile(i, carry):
            at = pl.ds(pl.multiple_of(row + i * 256, 256), 256)
            total = None
            for side in range(2):
                term = lax.dot_general(
                    w_ref[at, side * width:(side + 1) * width], cols[side, token, :],
                    (((1,), (1,)), ((), ())), preferred_element_type=jnp.float32,
                )
                total = term if total is None else total + term
            dst[pl.ds(pl.multiple_of(i * 256, 256), 256), :] = total.astype(dst.dtype)
            return carry

        lax.fori_loop(0, count // 256, tile, 0)

    to_core = [None] * 8

    def both(k):
        target = (place + TURNS[k] + 8) % 8
        product(ring_ctx(target, 1 - core), core_send.at[k])
        to_core[k] = send(core_send.at[k], core_recv.at[k], core_ssem.at[k], core_rsem.at[k], beside)
        product(ring_ctx(target, core), own.at[k])

    def mine(k, rows):
        return own[k, rows, :] + core_recv[k, rows, :].astype(jnp.float32)

    top, bottom, whole = slice(0, count // 2), slice(count // 2, count), slice(0, count)
    shares[0].wait_recv()
    both(0)
    shares[1].wait_recv()
    to_core[0].wait_recv()
    right_send[0, top, :] = mine(0, top).astype(jnp.bfloat16)
    left_send[0, bottom, :] = mine(0, bottom).astype(jnp.bfloat16)
    to_right = [send(right_send.at[0, top], right_recv.at[0, top], r_ssem.at[0], r_rsem.at[0], right)]
    to_left = [send(left_send.at[0, bottom], left_recv.at[0, bottom], l_ssem.at[0], l_rsem.at[0], left)]
    for k in (1, 2, 3, 4):
        both(k)
    for step in (1, 2, 3):
        k = 2 * step - 1
        to_core[k].wait_recv()
        to_right[step - 1].wait_recv()
        if step == 1:
            right_send[1, top, :] = (mine(k, top) + right_recv[0, top, :].astype(jnp.float32)).astype(jnp.bfloat16)
            right_send[1, bottom, :] = mine(k, bottom).astype(jnp.bfloat16)
        else:
            right_send[step] = (mine(k, whole) + right_recv[step - 1].astype(jnp.float32)).astype(jnp.bfloat16)
        to_right.append(send(right_send.at[step], right_recv.at[step], r_ssem.at[step], r_rsem.at[step], right))
        k += 1
        to_core[k].wait_recv()
        to_left[step - 1].wait_recv()
        if step == 1:
            left_send[1, top, :] = mine(k, top).astype(jnp.bfloat16)
            left_send[1, bottom, :] = (mine(k, bottom) + left_recv[0, bottom, :].astype(jnp.float32)).astype(jnp.bfloat16)
        else:
            left_send[step] = (mine(k, whole) + left_recv[step - 1].astype(jnp.float32)).astype(jnp.bfloat16)
        to_left.append(send(left_send.at[step], left_recv.at[step], l_ssem.at[step], l_rsem.at[step], left))
        if step == 1:
            for k in (5, 6, 7):
                both(k)
    to_core[7].wait_recv()
    to_right[3].wait_recv()
    to_left[3].wait_recv()
    total = mine(7, whole) + right_recv[3].astype(jnp.float32) + left_recv[3].astype(jnp.float32)
    last[...] = total.astype(jnp.bfloat16)

    @pl.when(near != tp)
    def _():
        end = send(last, landed, end_ssem, end_rsem, owner)
        end.wait()
        out_ref[...] = landed[...]

    @pl.when(near == tp)
    def _():
        out_ref[...] = last[...]

    for copy in shares + to_core + to_right + to_left:
        copy.wait_send()


def multiply_scatter(w_in, grad):
    rows, cols = w_in.shape
    seq_len, width = grad.shape
    block = rows // 8
    bf16 = functools.partial(pltpu.VMEM, dtype=jnp.bfloat16)
    dma = pltpu.SemaphoreType.DMA
    vmem = pl.BlockSpec(memory_space=pltpu.VMEM)
    return pl.pallas_call(
        scatter_kernel,
        out_shape=jax.ShapeDtypeStruct((block, block), jnp.bfloat16),
        in_specs=[vmem, pl.BlockSpec(memory_space=pl.ANY)],
        out_specs=vmem,
        scratch_shapes=[
            bf16((rows, cols)),
            bf16((2, seq_len, width)),
            pltpu.VMEM((8, block, block), jnp.float32),
            bf16((8, block, block)),
            bf16((8, block, block)),
            bf16((4, block, block)),
            bf16((4, block, block)),
            bf16((4, block, block)),
            bf16((4, block, block)),
            bf16((block, block)),
            bf16((block, block)),
            dma((2,)), dma((2,)), dma((2,)), dma((8,)), dma((8,)),
            dma((4,)), dma((4,)), dma((4,)), dma((4,)), dma, dma,
        ],
        compiler_params=pltpu.CompilerParams(
            collective_id=1, has_side_effects=True, vmem_limit_bytes=56 * 1024 * 1024
        ),
        cost_estimate=pl.CostEstimate(
            flops=2 * rows * cols * seq_len, bytes_accessed=2 * rows * cols, transcendentals=0
        ),
        name="multiply_scatter",
    )(grad, w_in)


def gather_kernel(tokens_ref, w_hbm, proj_ref, w_ref, pieces, total, part_send, part_recv, local_sem,
                  swap_ssem, swap_rsem, core_ssem, core_rsem, r_ssem, r_rsem, l_ssem, l_rsem, x_ssem, x_rsem):
    ctx, tp = lax.axis_index("ctx"), lax.axis_index("tp")
    core, place = ctx % 2, ring_place(ctx)
    across = (ctx, 1 - tp)
    beside = (ctx + 1 - 2 * core, tp)
    right = (ring_ctx((place + 1) % 8, core), tp)
    left = (ring_ctx((place + 7) % 8, core), tp)
    owner = (tp * 8 + ctx % 8, ctx // 8)
    near = ctx // 8
    count, width = tokens_ref.shape[0], proj_ref.shape[1]
    load = pltpu.make_async_copy(w_hbm, w_ref, local_sem.at[0])
    load.start()
    greet([across, beside, right, left], owner, ctx, tp)

    def send(src, dst, ssem, rsem, where):
        copy = pltpu.make_async_remote_copy(
            src_ref=src, dst_ref=dst, send_sem=ssem, recv_sem=rsem, device_id=where, device_id_type=MESH
        )
        copy.start()
        return copy

    def pass_on(place_of, ssem, rsem, where, rows=None):
        piece = ring_ctx(place_of, core)
        ref = pieces.at[piece] if rows is None else pieces.at[piece, rows]
        return send(ref, ref, ssem, rsem, where)

    def at_place(turn):
        return (place + turn + 8) % 8

    @pl.when(near != tp)
    def _():
        swap = send(tokens_ref, pieces.at[owner[0]], swap_ssem, swap_rsem, owner)
        total[...] = jnp.zeros_like(total)
        swap.wait()

    @pl.when(near == tp)
    def _():
        keep = pltpu.make_async_copy(tokens_ref, pieces.at[ctx], local_sem.at[1])
        keep.start()
        keep.wait()

    to_right = [pass_on(place, r_ssem.at[0], r_rsem.at[0], right)]
    to_left = [pass_on(place, l_ssem.at[0], l_rsem.at[0], left)]
    to_core = [pass_on(place, core_ssem.at[0], core_rsem.at[0], beside)]

    @pl.when(near == tp)
    def _():
        total[...] = jnp.zeros_like(total)

    load.wait()

    def add(piece, side):
        row = pl.ds(pl.multiple_of((piece % 8) * count, count), count)
        lanes = pl.ds(pl.multiple_of(side * width, LANES), width)
        token = (piece // 8) * count

        def tile(i, carry):
            at = pl.ds(pl.multiple_of(token + i * 256, 256), 256)
            block = pieces[piece, pl.ds(pl.multiple_of(i * 256, 256), 256), :]
            total[side, at, :] += jnp.dot(block, w_ref[row, lanes], preferred_element_type=jnp.float32)
            return carry

        lax.fori_loop(0, count // 256, tile, 0)

    def add_place(turn, whose):
        for side in range(2):
            add(ring_ctx(at_place(turn), whose), side)

    add_place(0, core)
    top, bottom = slice(0, count // 2), slice(count // 2, count)
    for step in (1, 2, 3):
        to_right[step - 1].wait_recv()
        to_right.append(pass_on(at_place(-step), r_ssem.at[step], r_rsem.at[step], right, top if step == 3 else None))
        to_core.append(pass_on(at_place(-step), core_ssem.at[2 * step - 1], core_rsem.at[2 * step - 1], beside))
        to_left[step - 1].wait_recv()
        to_left.append(pass_on(at_place(step), l_ssem.at[step], l_rsem.at[step], left, bottom if step == 3 else None))
        to_core.append(pass_on(at_place(step), core_ssem.at[2 * step], core_rsem.at[2 * step], beside))
        add_place(-step, core)
        add_place(step, core)
        if step == 1:
            to_core[0].wait_recv()
            add_place(0, 1 - core)
        to_core[2 * step - 1].wait_recv()
        add_place(-step, 1 - core)
        to_core[2 * step].wait_recv()
        add_place(step, 1 - core)

    def rows_of(half):
        return pl.ds(pl.multiple_of(half * count, count), count)

    def share(turn, half):
        at = rows_of(half)
        part_send[at, :] = total[1 - tp, at, :].astype(jnp.bfloat16)
        return send(part_send.at[at], part_recv.at[at], x_ssem.at[turn], x_rsem.at[turn], across)

    shares = [share(0, near)]
    to_right[3].wait_recv()
    to_left[3].wait_recv()
    to_core.append(pass_on(at_place(4), core_ssem.at[7], core_rsem.at[7], beside))
    mine, theirs = ring_ctx(at_place(4), core), ring_ctx(at_place(4), 1 - core)
    add(mine, 1 - tp)
    to_core[7].wait_recv()
    add(theirs, 1 - tp)
    shares.append(share(1, 1 - near))
    add(mine, tp)
    add(theirs, tp)
    for turn, half in enumerate((near, 1 - near)):
        at = rows_of(half)
        shares[turn].wait_recv()
        proj_ref[at, :] = (total[tp, at, :] + part_recv[at, :].astype(jnp.float32)).astype(jnp.bfloat16)
    for copy in shares + to_core + to_right + to_left:
        copy.wait_send()


def gather_multiply(tokens, w_in):
    rows, cols = w_in.shape
    count, depth = tokens.shape
    seq_len, width = 2 * count, cols // 2
    bf16 = functools.partial(pltpu.VMEM, dtype=jnp.bfloat16)
    dma = pltpu.SemaphoreType.DMA
    vmem = pl.BlockSpec(memory_space=pltpu.VMEM)
    return pl.pallas_call(
        gather_kernel,
        out_shape=jax.ShapeDtypeStruct((seq_len, width), jnp.bfloat16),
        in_specs=[vmem, pl.BlockSpec(memory_space=pl.ANY)],
        out_specs=vmem,
        scratch_shapes=[
            bf16((rows, cols)),
            bf16((16, count, depth)),
            pltpu.VMEM((2, seq_len, width), jnp.float32),
            bf16((seq_len, width)),
            bf16((seq_len, width)),
            dma((2,)), dma, dma, dma((8,)), dma((8,)),
            dma((4,)), dma((4,)), dma((4,)), dma((4,)), dma((2,)), dma((2,)),
        ],
        compiler_params=pltpu.CompilerParams(
            collective_id=0, has_side_effects=True, vmem_limit_bytes=56 * 1024 * 1024
        ),
        cost_estimate=pl.CostEstimate(
            flops=2 * rows * cols * seq_len, bytes_accessed=2 * rows * cols, transcendentals=0
        ),
        name="gather_multiply",
    )(tokens, w_in)


def mix_kernel(seq_len, chans, modes, chunks, proj_ref, spread_ref, taps_ref, rate_ref, res_ref,
               cot_ref, mixed_ref, grad_ref, planes, feats, sums, grads, outs, backs, rates, powers):
    halves = chans // LANES
    rows = chunks * halves
    steps = seq_len // chunks
    tile = steps

    def multiply(i, carry):
        at = pl.ds(pl.multiple_of(i * tile, tile), tile)
        planes[at, :] = jnp.dot(proj_ref[at, :], spread_ref[...], preferred_element_type=jnp.float32)
        return carry

    lax.fori_loop(0, chunks, multiply, 0)

    row_id = lax.broadcasted_iota(jnp.int32, (seq_len, LANES), 0)
    taps_count = taps_ref.shape[0]
    for col in range(3 * halves):
        lanes = slice(col * LANES, (col + 1) * LANES)
        plane = planes[:, lanes]
        total = plane * taps_ref[0:1, lanes]
        for delay in range(1, taps_count):
            shifted = jnp.where(row_id >= delay, pltpu.roll(plane, delay, 0), 0.0)
            total = total + shifted * taps_ref[delay:delay + 1, lanes]
        feats[:, lanes] = total

    for half in range(halves):
        lanes = [slice((r * halves + half) * LANES, (r * halves + half + 1) * LANES) for r in range(3)]
        for chunk in range(chunks):
            at = slice(chunk * steps, (chunk + 1) * steps)
            row = pl.ds(chunk * halves + half, steps, stride=rows)
            sums[row, :] = feats[at, lanes[1]] * feats[at, lanes[2]]
            cot = cot_ref[half * LANES:(half + 1) * LANES, at].astype(jnp.float32).T
            planes[at, half * LANES:(half + 1) * LANES] = cot
            grads[row, :] = cot * feats[at, lanes[0]]

    chunk_id = lax.broadcasted_iota(jnp.int32, (rows, LANES), 0) // halves
    for m in range(modes):
        rates[m] = jnp.exp(-rate_ref[m])
        powers[m] = jnp.exp(-rate_ref[m] * float(steps))

    def scan(source, result, backward):
        def place(step):
            at = steps - 1 - step if backward else step
            return pl.ds(pl.multiple_of(at * rows, rows), rows)

        def ends(step, states):
            u = source[place(step), :]
            return tuple(rates[m] * states[m] + u for m in range(modes))

        zeros = tuple(jnp.zeros((rows, LANES), jnp.float32) for _ in range(modes))
        last = lax.fori_loop(0, steps, ends, zeros, unroll=4)
        first = []
        for m in range(modes):
            carry = jnp.zeros((rows, LANES), jnp.float32)
            for _ in range(chunks - 1):
                total = powers[m] * carry + last[m]
                if backward:
                    carry = jnp.where(chunk_id < chunks - 1, pltpu.roll(total, rows - halves, 0), 0.0)
                else:
                    carry = jnp.where(chunk_id > 0, pltpu.roll(total, halves, 0), 0.0)
            first.append(carry)

        def run(step, states):
            u = source[place(step), :]
            states = tuple(rates[m] * states[m] + u for m in range(modes))
            terms = [res_ref[m] * states[m] for m in range(modes)]
            while len(terms) > 1:
                terms = [a + b for a, b in zip(terms[0::2], terms[1::2])]
            result[place(step), :] = terms[0]
            return states

        lax.fori_loop(0, steps, run, tuple(first), unroll=4)

    scan(sums, outs, False)
    scan(grads, backs, True)

    for half in range(halves):
        lanes = [slice((r * halves + half) * LANES, (r * halves + half + 1) * LANES) for r in range(3)]
        for chunk in range(chunks):
            at = slice(chunk * steps, (chunk + 1) * steps)
            row = pl.ds(chunk * halves + half, steps, stride=rows)
            y = outs[row, :]
            du = backs[row, :]
            mixed_ref[half * LANES:(half + 1) * LANES, at] = (feats[at, lanes[0]] * y).T.astype(jnp.bfloat16)
            cot = planes[at, half * LANES:(half + 1) * LANES]
            key = feats[at, lanes[1]]
            feats[at, lanes[0]] = cot * y
            feats[at, lanes[1]] = du * feats[at, lanes[2]]
            feats[at, lanes[2]] = du * key

    for col in range(3 * halves):
        lanes = slice(col * LANES, (col + 1) * LANES)
        grad = feats[:, lanes]
        total = grad * taps_ref[0:1, lanes]
        for delay in range(1, taps_count):
            shifted = jnp.where(row_id < seq_len - delay, pltpu.roll(grad, seq_len - delay, 0), 0.0)
            total = total + shifted * taps_ref[delay:delay + 1, lanes]
        planes[:, lanes] = total

    def gather(i, carry):
        at = pl.ds(pl.multiple_of(i * tile, tile), tile)
        grad_ref[at, :] = lax.dot_general(
            planes[at, :].astype(jnp.bfloat16), spread_ref[...], (((1,), (1,)), ((), ())),
            preferred_element_type=jnp.float32,
        ).astype(jnp.bfloat16)
        return carry

    lax.fori_loop(0, chunks, gather, 0)


def mix(projected, short_taps, li_residue, li_rate, cotangent):
    seq_len, cols = projected.shape
    chans, modes = li_rate.shape
    halves = chans // LANES
    rows = 8
    chunks = rows // halves
    source = jnp.arange(cols)[:, None]
    target = jnp.arange(cols)[None, :]
    spread = (source == 3 * (target % chans) + target // chans).astype(jnp.bfloat16)
    taps = short_taps.reshape(-1, chans, 3).transpose(0, 2, 1).reshape(-1, cols)

    def per_row(values):
        return jnp.tile(values.T.reshape(modes, halves, LANES), (1, chunks, 1))

    f32 = functools.partial(pltpu.VMEM, dtype=jnp.float32)
    vmem = pl.BlockSpec(memory_space=pltpu.VMEM)
    return pl.pallas_call(
        functools.partial(mix_kernel, seq_len, chans, modes, chunks),
        out_shape=(
            jax.ShapeDtypeStruct((chans, seq_len), jnp.bfloat16),
            jax.ShapeDtypeStruct((seq_len, cols), jnp.bfloat16),
        ),
        in_specs=[vmem] * 6,
        out_specs=(vmem, vmem),
        scratch_shapes=[
            f32((seq_len, cols)),
            f32((seq_len, cols)),
            f32((seq_len * halves, LANES)),
            f32((seq_len * halves, LANES)),
            f32((seq_len * halves, LANES)),
            f32((seq_len * halves, LANES)),
            f32((modes, rows, LANES)),
            f32((modes, rows, LANES)),
        ],
        compiler_params=pltpu.CompilerParams(vmem_limit_bytes=40 * 1024 * 1024),
        cost_estimate=pl.CostEstimate(
            flops=20 * 10**9, bytes_accessed=6 * seq_len * cols, transcendentals=0
        ),
        name="mix",
    )(projected, spread, taps, per_row(li_rate), per_row(li_residue), cotangent)


def fast_shards(tokens, w_in, short_taps, li_residue, li_rate, cotangent):
    projected = gather_multiply(tokens, w_in)
    mixed, grad = mix(projected, short_taps, li_residue, li_rate, cotangent)
    return mixed, multiply_scatter(w_in, grad)


def solution(mesh):
    n_ctx, n_tp = mesh.shape["ctx"], mesh.shape["tp"]
    body = fast_shards if (n_ctx, n_tp) == (16, 2) else shards
    in_specs = (
        P("tp", "ctx"),
        P("tp", "ctx"),
        P(None, ("ctx", "tp")),
        P(("ctx", "tp"), None),
        P(("ctx", "tp"), None),
        P(("ctx", "tp"), None),
    )
    out_specs = (P(("ctx", "tp"), None), P("ctx", "tp"))
    return jax.shard_map(body, mesh=mesh, in_specs=in_specs, out_specs=out_specs, check_vma=False)
```

```python
import functools
import math

import jax
import jax.numpy as jnp
from jax import lax
from jax.experimental import pallas as pl
from jax.experimental.pallas import tpu as pltpu
from jax.sharding import PartitionSpec as P

HIGH = lax.Precision.HIGHEST
LANES = 128


def causal_taps(signal, taps):
    seq_len = signal.shape[0]
    features = signal * taps[0]
    for delay in range(1, taps.shape[0]):
        shifted = jnp.concatenate(
            [jnp.zeros((delay, signal.shape[1]), signal.dtype), signal[: seq_len - delay]], axis=0
        )
        features = features + shifted * taps[delay]
    return features


def long_filter(signal, residue, decay):
    chan_count, seq_len = signal.shape
    tile_size = math.gcd(seq_len, 128)
    tile_count = seq_len // tile_size
    tiled = signal.reshape(chan_count, tile_count, tile_size)
    offsets = jnp.arange(tile_size, dtype=jnp.float32)
    head_taps = jnp.einsum(
        "cm,cml->cl", residue, jnp.exp(-decay[:, :, None] * offsets[None, None, :]), precision=HIGH
    )
    distance = jnp.arange(tile_size)[:, None] - jnp.arange(tile_size)[None, :]
    clipped = jnp.maximum(distance, 0)
    current = jnp.where(distance >= 0, head_taps[:, clipped], 0.0)
    inside = jnp.einsum("cts,cbs->cbt", current, tiled, precision=HIGH)
    end_decay = jnp.exp(-decay[:, :, None] * (tile_size - 1.0 - offsets)[None, None, :])
    states = jnp.einsum("cbt,cmt->cmb", tiled, end_decay, precision=HIGH)
    tile_index = jnp.arange(tile_count)
    tile_gap = tile_index[:, None] - 1 - tile_index[None, :]
    spans = (tile_size * jnp.maximum(tile_gap, 0)).astype(jnp.float32)
    carry_weight = jnp.where(tile_gap >= 0, jnp.exp(-decay[:, :, None, None] * spans), 0.0)
    carried = jnp.einsum("cmbk,cmk->cmb", carry_weight, states, precision=HIGH)
    start_decay = jnp.exp(-decay[:, :, None] * (offsets + 1.0)[None, None, :])
    across = jnp.einsum("cm,cmb,cmt->cbt", residue, carried, start_decay, precision=HIGH)
    return (inside + across).reshape(chan_count, seq_len)


def mixer(signal, taps, residue, decay):
    seq_len = signal.shape[0]
    chan_count = residue.shape[0]
    features = causal_taps(signal, taps).reshape(seq_len, chan_count, 3)
    query_part = features[:, :, 0].T
    key_part = features[:, :, 1].T
    value_part = features[:, :, 2].T
    return query_part * long_filter(key_part * value_part, residue, decay)


def shards(tokens, w_in, short_taps, li_residue, li_rate, cotangent):
    features = lax.all_gather(tokens, "ctx", axis=1, tiled=True)
    weights = lax.all_gather(w_in, "tp", axis=0, tiled=True)
    projected = jnp.dot(features, weights, preferred_element_type=jnp.float32)
    rounded = projected.astype(jnp.bfloat16)
    channels = lax.all_to_all(rounded, "tp", split_axis=1, concat_axis=0, tiled=True)
    signal = channels.astype(jnp.float32)

    def local_mix(given):
        return mixer(given, short_taps, li_residue, li_rate)

    mixed_out, pullback = jax.vjp(local_mix, signal)
    grad_signal = pullback(cotangent.astype(jnp.float32))[0]
    grad_rounded = grad_signal.astype(jnp.bfloat16)
    grad_rows = lax.all_to_all(grad_rounded, "tp", split_axis=0, concat_axis=1, tiled=True)
    summed = lax.psum_scatter(
        lax.dot_general(
            weights, grad_rows, (((1,), (1,)), ((), ())), preferred_element_type=jnp.float32
        ).astype(jnp.bfloat16),
        "ctx",
        scatter_dimension=0,
        tiled=True,
    )
    return (mixed_out.astype(jnp.bfloat16), summed)


MESH = pl.DeviceIdType.MESH
TURNS = (4, 3, -3, 2, -2, 1, -1, 0)


def ring_place(ctx):
    z, y = ctx // 4, (ctx // 2) % 2
    return z + y * (7 - 2 * z)


def ring_ctx(place, core):
    y = place // 4
    z = place + y * (7 - 2 * place)
    return z * 4 + y * 2 + core


def greet(others, partner, ctx, tp):
    barrier = pltpu.get_barrier_semaphore()
    for other in others:
        pl.semaphore_signal(barrier, inc=1, device_id=other, device_id_type=MESH)

    @pl.when(ctx // 8 != tp)
    def _():
        pl.semaphore_signal(barrier, inc=1, device_id=partner, device_id_type=MESH)
        pl.semaphore_wait(barrier, len(others) + 1)

    @pl.when(ctx // 8 == tp)
    def _():
        pl.semaphore_wait(barrier, len(others))


def scatter_kernel(grad_ref, w_hbm, out_ref, w_ref, cols, own, core_send, core_recv, right_send, right_recv,
                   left_send, left_recv, last, landed, local_sem, x_ssem, x_rsem, core_ssem, core_rsem,
                   r_ssem, r_rsem, l_ssem, l_rsem, end_ssem, end_rsem):
    ctx, tp = lax.axis_index("ctx"), lax.axis_index("tp")
    core, place = ctx % 2, ring_place(ctx)
    across = (ctx, 1 - tp)
    beside = (ctx + 1 - 2 * core, tp)
    right = (ring_ctx((place + 1) % 8, core), tp)
    left = (ring_ctx((place + 7) % 8, core), tp)
    owner = (tp * 8 + ctx % 8, ctx // 8)
    count, width = own.shape[2], grad_ref.shape[1]
    load = pltpu.make_async_copy(w_hbm, w_ref, local_sem.at[0])
    load.start()
    keep = pltpu.make_async_copy(grad_ref, cols.at[tp], local_sem.at[1])
    keep.start()
    greet([across, beside, right, left], owner, ctx, tp)

    def send(src, dst, ssem, rsem, where):
        copy = pltpu.make_async_remote_copy(
            src_ref=src, dst_ref=dst, send_sem=ssem, recv_sem=rsem, device_id=where, device_id_type=MESH
        )
        copy.start()
        return copy

    near = ctx // 8
    shares = []
    for turn, half in enumerate((1 - near, near)):
        at = pl.ds(pl.multiple_of(half * count, count), count)
        shares.append(send(grad_ref.at[at], cols.at[tp, at], x_ssem.at[turn], x_rsem.at[turn], across))
    load.wait()
    keep.wait()

    def product(piece, dst):
        row = (piece % 8) * count
        token = pl.ds(pl.multiple_of((piece // 8) * count, count), count)

        def tile(i, carry):
            at = pl.ds(pl.multiple_of(row + i * 256, 256), 256)
            total = None
            for side in range(2):
                term = lax.dot_general(
                    w_ref[at, side * width:(side + 1) * width], cols[side, token, :],
                    (((1,), (1,)), ((), ())), preferred_element_type=jnp.float32,
                )
                total = term if total is None else total + term
            dst[pl.ds(pl.multiple_of(i * 256, 256), 256), :] = total.astype(dst.dtype)
            return carry

        lax.fori_loop(0, count // 256, tile, 0)

    to_core = [None] * 8

    def both(k):
        target = (place + TURNS[k] + 8) % 8
        product(ring_ctx(target, 1 - core), core_send.at[k])
        to_core[k] = send(core_send.at[k], core_recv.at[k], core_ssem.at[k], core_rsem.at[k], beside)
        product(ring_ctx(target, core), own.at[k])

    def mine(k, rows):
        return own[k, rows, :] + core_recv[k, rows, :].astype(jnp.float32)

    top, bottom, whole = slice(0, count // 2), slice(count // 2, count), slice(0, count)
    shares[0].wait_recv()
    both(0)
    shares[1].wait_recv()
    to_core[0].wait_recv()
    right_send[0, top, :] = mine(0, top).astype(jnp.bfloat16)
    left_send[0, bottom, :] = mine(0, bottom).astype(jnp.bfloat16)
    to_right = {(0, 0): send(right_send.at[0, top], right_recv.at[0, top], r_ssem.at[0, 0], r_rsem.at[0, 0], right)}
    to_left = {(0, 1): send(left_send.at[0, bottom], left_recv.at[0, bottom], l_ssem.at[0, 1], l_rsem.at[0, 1], left)}
    for k in (1, 2, 3, 4):
        both(k)
    sides = (top, bottom)

    def relay(step, side, k, sent, out, got, ssem, rsem, where):
        rows = sides[side]
        value = mine(k, rows)
        if (step - 1, side) in sent:
            sent[step - 1, side].wait_recv()
            value = value + got[step - 1, rows, :].astype(jnp.float32)
        out[step, rows, :] = value.astype(jnp.bfloat16)
        sent[step, side] = send(
            out.at[step, rows], got.at[step, rows], ssem.at[step, side], rsem.at[step, side], where
        )

    for step in (1, 2, 3):
        to_core[2 * step - 1].wait_recv()
        to_core[2 * step].wait_recv()
        for side in range(2):
            relay(step, 1 - side, 2 * step - 1, to_right, right_send, right_recv, r_ssem, r_rsem, right)
            relay(step, side, 2 * step, to_left, left_send, left_recv, l_ssem, l_rsem, left)
        if step == 1:
            for k in (5, 6, 7):
                both(k)
    to_core[7].wait_recv()

    def ending(side):
        rows = sides[side]
        return pltpu.make_async_remote_copy(
            src_ref=last.at[rows], dst_ref=landed.at[rows], send_sem=end_ssem.at[side],
            recv_sem=end_rsem.at[side], device_id=owner, device_id_type=MESH,
        )

    to_right[3, 1].wait_recv()
    to_left[3, 0].wait_recv()
    for side in range(2):
        rows = sides[side]
        if side == 0:
            to_right[3, 0].wait_recv()
        else:
            to_left[3, 1].wait_recv()
        total = mine(7, rows) + right_recv[3, rows, :].astype(jnp.float32) + left_recv[3, rows, :].astype(jnp.float32)
        last[rows, :] = total.astype(jnp.bfloat16)

        @pl.when(near != tp)
        def _():
            ending(side).start()

    @pl.when(near != tp)
    def _():
        for side in range(2):
            ending(side).wait()
            out_ref[sides[side], :] = landed[sides[side], :]

    @pl.when(near == tp)
    def _():
        out_ref[...] = last[...]

    for copy in shares + to_core + list(to_right.values()) + list(to_left.values()):
        copy.wait_send()


def multiply_scatter(w_in, grad):
    rows, cols = w_in.shape
    seq_len, width = grad.shape
    block = rows // 8
    bf16 = functools.partial(pltpu.VMEM, dtype=jnp.bfloat16)
    dma = pltpu.SemaphoreType.DMA
    vmem = pl.BlockSpec(memory_space=pltpu.VMEM)
    return pl.pallas_call(
        scatter_kernel,
        out_shape=jax.ShapeDtypeStruct((block, block), jnp.bfloat16),
        in_specs=[vmem, pl.BlockSpec(memory_space=pl.ANY)],
        out_specs=vmem,
        scratch_shapes=[
            bf16((rows, cols)),
            bf16((2, seq_len, width)),
            pltpu.VMEM((8, block, block), jnp.float32),
            bf16((8, block, block)),
            bf16((8, block, block)),
            bf16((4, block, block)),
            bf16((4, block, block)),
            bf16((4, block, block)),
            bf16((4, block, block)),
            bf16((block, block)),
            bf16((block, block)),
            dma((2,)), dma((2,)), dma((2,)), dma((8,)), dma((8,)),
            dma((4, 2)), dma((4, 2)), dma((4, 2)), dma((4, 2)), dma((2,)), dma((2,)),
        ],
        compiler_params=pltpu.CompilerParams(
            collective_id=1, has_side_effects=True, vmem_limit_bytes=56 * 1024 * 1024
        ),
        cost_estimate=pl.CostEstimate(
            flops=2 * rows * cols * seq_len, bytes_accessed=2 * rows * cols, transcendentals=0
        ),
        name="multiply_scatter",
    )(grad, w_in)


def gather_kernel(tokens_ref, w_hbm, proj_ref, w_ref, pieces, total, part_send, part_recv, local_sem,
                  swap_ssem, swap_rsem, core_ssem, core_rsem, r_ssem, r_rsem, l_ssem, l_rsem, x_ssem, x_rsem):
    ctx, tp = lax.axis_index("ctx"), lax.axis_index("tp")
    core, place = ctx % 2, ring_place(ctx)
    across = (ctx, 1 - tp)
    beside = (ctx + 1 - 2 * core, tp)
    right = (ring_ctx((place + 1) % 8, core), tp)
    left = (ring_ctx((place + 7) % 8, core), tp)
    owner = (tp * 8 + ctx % 8, ctx // 8)
    near = ctx // 8
    count, width = tokens_ref.shape[0], proj_ref.shape[1]
    load = pltpu.make_async_copy(w_hbm, w_ref, local_sem.at[0])
    load.start()
    greet([across, beside, right, left], owner, ctx, tp)

    def send(src, dst, ssem, rsem, where):
        copy = pltpu.make_async_remote_copy(
            src_ref=src, dst_ref=dst, send_sem=ssem, recv_sem=rsem, device_id=where, device_id_type=MESH
        )
        copy.start()
        return copy

    top, bottom = slice(0, count // 2), slice(count // 2, count)
    sides = (top, bottom)

    def pass_on(place_of, ssem, rsem, where, side=None):
        piece = ring_ctx(place_of, core)
        ref = pieces.at[piece] if side is None else pieces.at[piece, sides[side]]
        return send(ref, ref, ssem, rsem, where)

    def at_place(turn):
        return (place + turn + 8) % 8

    def swap(side):
        return pltpu.make_async_remote_copy(
            src_ref=tokens_ref.at[sides[side]], dst_ref=pieces.at[owner[0], sides[side]],
            send_sem=swap_ssem.at[side], recv_sem=swap_rsem.at[side], device_id=owner, device_id_type=MESH,
        )

    @pl.when(near != tp)
    def _():
        swap(0).start()
        swap(1).start()
        total[...] = jnp.zeros_like(total)

    @pl.when(near == tp)
    def _():
        keep = pltpu.make_async_copy(tokens_ref, pieces.at[ctx], local_sem.at[1])
        keep.start()
        keep.wait()

    to_right, to_left = {}, {}
    for side in range(2):
        @pl.when(near != tp)
        def _():
            swap(side).wait()

        to_right[0, side] = pass_on(place, r_ssem.at[0, side], r_rsem.at[0, side], right, side)
        to_left[0, side] = pass_on(place, l_ssem.at[0, side], l_rsem.at[0, side], left, side)
    to_core = [pass_on(place, core_ssem.at[0], core_rsem.at[0], beside)]

    @pl.when(near == tp)
    def _():
        total[...] = jnp.zeros_like(total)

    load.wait()

    def add(piece, side):
        row = pl.ds(pl.multiple_of((piece % 8) * count, count), count)
        lanes = pl.ds(pl.multiple_of(side * width, LANES), width)
        token = (piece // 8) * count

        def tile(i, carry):
            at = pl.ds(pl.multiple_of(token + i * 256, 256), 256)
            block = pieces[piece, pl.ds(pl.multiple_of(i * 256, 256), 256), :]
            total[side, at, :] += jnp.dot(block, w_ref[row, lanes], preferred_element_type=jnp.float32)
            return carry

        lax.fori_loop(0, count // 256, tile, 0)

    def add_place(turn, whose):
        for side in range(2):
            add(ring_ctx(at_place(turn), whose), side)

    add_place(0, core)
    for step in (1, 2, 3):
        for side in range(2):
            to_right[step - 1, side].wait_recv()
            if step < 3 or side == 0:
                to_right[step, side] = pass_on(
                    at_place(-step), r_ssem.at[step, side], r_rsem.at[step, side], right, side
                )
            to_left[step - 1, side].wait_recv()
            if step < 3 or side == 1:
                to_left[step, side] = pass_on(
                    at_place(step), l_ssem.at[step, side], l_rsem.at[step, side], left, side
                )
        to_core.append(pass_on(at_place(-step), core_ssem.at[2 * step - 1], core_rsem.at[2 * step - 1], beside))
        to_core.append(pass_on(at_place(step), core_ssem.at[2 * step], core_rsem.at[2 * step], beside))
        add_place(-step, core)
        add_place(step, core)
        if step == 1:
            to_core[0].wait_recv()
            add_place(0, 1 - core)
        to_core[2 * step - 1].wait_recv()
        add_place(-step, 1 - core)
        to_core[2 * step].wait_recv()
        add_place(step, 1 - core)

    def rows_of(half):
        return pl.ds(pl.multiple_of(half * count, count), count)

    def share(turn, half):
        at = rows_of(half)
        part_send[at, :] = total[1 - tp, at, :].astype(jnp.bfloat16)
        return send(part_send.at[at], part_recv.at[at], x_ssem.at[turn], x_rsem.at[turn], across)

    shares = [share(0, near)]
    to_right[3, 0].wait_recv()
    to_left[3, 1].wait_recv()
    to_core.append(pass_on(at_place(4), core_ssem.at[7], core_rsem.at[7], beside))
    mine, theirs = ring_ctx(at_place(4), core), ring_ctx(at_place(4), 1 - core)
    add(mine, 1 - tp)
    to_core[7].wait_recv()
    add(theirs, 1 - tp)
    shares.append(share(1, 1 - near))
    add(mine, tp)
    add(theirs, tp)
    for turn, half in enumerate((near, 1 - near)):
        at = rows_of(half)
        shares[turn].wait_recv()
        proj_ref[at, :] = (total[tp, at, :] + part_recv[at, :].astype(jnp.float32)).astype(jnp.bfloat16)
    for copy in shares + to_core + list(to_right.values()) + list(to_left.values()):
        copy.wait_send()


def gather_multiply(tokens, w_in):
    rows, cols = w_in.shape
    count, depth = tokens.shape
    seq_len, width = 2 * count, cols // 2
    bf16 = functools.partial(pltpu.VMEM, dtype=jnp.bfloat16)
    dma = pltpu.SemaphoreType.DMA
    vmem = pl.BlockSpec(memory_space=pltpu.VMEM)
    return pl.pallas_call(
        gather_kernel,
        out_shape=jax.ShapeDtypeStruct((seq_len, width), jnp.bfloat16),
        in_specs=[vmem, pl.BlockSpec(memory_space=pl.ANY)],
        out_specs=vmem,
        scratch_shapes=[
            bf16((rows, cols)),
            bf16((16, count, depth)),
            pltpu.VMEM((2, seq_len, width), jnp.float32),
            bf16((seq_len, width)),
            bf16((seq_len, width)),
            dma((2,)), dma((2,)), dma((2,)), dma((8,)), dma((8,)),
            dma((4, 2)), dma((4, 2)), dma((4, 2)), dma((4, 2)), dma((2,)), dma((2,)),
        ],
        compiler_params=pltpu.CompilerParams(
            collective_id=0, has_side_effects=True, vmem_limit_bytes=56 * 1024 * 1024
        ),
        cost_estimate=pl.CostEstimate(
            flops=2 * rows * cols * seq_len, bytes_accessed=2 * rows * cols, transcendentals=0
        ),
        name="gather_multiply",
    )(tokens, w_in)


def mix_kernel(seq_len, chans, modes, chunks, proj_ref, spread_ref, taps_ref, rate_ref, res_ref,
               cot_ref, mixed_ref, grad_ref, planes, feats, sums, grads, outs, backs, rates, powers):
    halves = chans // LANES
    rows = chunks * halves
    steps = seq_len // chunks
    tile = steps

    def multiply(i, carry):
        at = pl.ds(pl.multiple_of(i * tile, tile), tile)
        planes[at, :] = jnp.dot(proj_ref[at, :], spread_ref[...], preferred_element_type=jnp.float32)
        return carry

    lax.fori_loop(0, chunks, multiply, 0)

    row_id = lax.broadcasted_iota(jnp.int32, (seq_len, LANES), 0)
    taps_count = taps_ref.shape[0]
    for col in range(3 * halves):
        lanes = slice(col * LANES, (col + 1) * LANES)
        plane = planes[:, lanes]
        total = plane * taps_ref[0:1, lanes]
        for delay in range(1, taps_count):
            shifted = jnp.where(row_id >= delay, pltpu.roll(plane, delay, 0), 0.0)
            total = total + shifted * taps_ref[delay:delay + 1, lanes]
        feats[:, lanes] = total

    for half in range(halves):
        lanes = [slice((r * halves + half) * LANES, (r * halves + half + 1) * LANES) for r in range(3)]
        for chunk in range(chunks):
            at = slice(chunk * steps, (chunk + 1) * steps)
            row = pl.ds(chunk * halves + half, steps, stride=rows)
            sums[row, :] = feats[at, lanes[1]] * feats[at, lanes[2]]
            cot = cot_ref[half * LANES:(half + 1) * LANES, at].astype(jnp.float32).T
            planes[at, half * LANES:(half + 1) * LANES] = cot
            grads[row, :] = cot * feats[at, lanes[0]]

    chunk_id = lax.broadcasted_iota(jnp.int32, (rows, LANES), 0) // halves
    for m in range(modes):
        rates[m] = jnp.exp(-rate_ref[m])
        powers[m] = jnp.exp(-rate_ref[m] * float(steps))

    def scan(source, result, backward):
        def place(step):
            at = steps - 1 - step if backward else step
            return pl.ds(pl.multiple_of(at * rows, rows), rows)

        def ends(step, states):
            u = source[place(step), :]
            return tuple(rates[m] * states[m] + u for m in range(modes))

        zeros = tuple(jnp.zeros((rows, LANES), jnp.float32) for _ in range(modes))
        last = lax.fori_loop(0, steps, ends, zeros, unroll=4)
        first = []
        for m in range(modes):
            carry = jnp.zeros((rows, LANES), jnp.float32)
            for _ in range(chunks - 1):
                total = powers[m] * carry + last[m]
                if backward:
                    carry = jnp.where(chunk_id < chunks - 1, pltpu.roll(total, rows - halves, 0), 0.0)
                else:
                    carry = jnp.where(chunk_id > 0, pltpu.roll(total, halves, 0), 0.0)
            first.append(carry)

        def run(step, states):
            u = source[place(step), :]
            states = tuple(rates[m] * states[m] + u for m in range(modes))
            terms = [res_ref[m] * states[m] for m in range(modes)]
            while len(terms) > 1:
                terms = [a + b for a, b in zip(terms[0::2], terms[1::2])]
            result[place(step), :] = terms[0]
            return states

        lax.fori_loop(0, steps, run, tuple(first), unroll=4)

    scan(sums, outs, False)
    scan(grads, backs, True)

    for half in range(halves):
        lanes = [slice((r * halves + half) * LANES, (r * halves + half + 1) * LANES) for r in range(3)]
        for chunk in range(chunks):
            at = slice(chunk * steps, (chunk + 1) * steps)
            row = pl.ds(chunk * halves + half, steps, stride=rows)
            y = outs[row, :]
            du = backs[row, :]
            mixed_ref[half * LANES:(half + 1) * LANES, at] = (feats[at, lanes[0]] * y).T.astype(jnp.bfloat16)
            cot = planes[at, half * LANES:(half + 1) * LANES]
            key = feats[at, lanes[1]]
            feats[at, lanes[0]] = cot * y
            feats[at, lanes[1]] = du * feats[at, lanes[2]]
            feats[at, lanes[2]] = du * key

    for col in range(3 * halves):
        lanes = slice(col * LANES, (col + 1) * LANES)
        grad = feats[:, lanes]
        total = grad * taps_ref[0:1, lanes]
        for delay in range(1, taps_count):
            shifted = jnp.where(row_id < seq_len - delay, pltpu.roll(grad, seq_len - delay, 0), 0.0)
            total = total + shifted * taps_ref[delay:delay + 1, lanes]
        planes[:, lanes] = total

    def gather(i, carry):
        at = pl.ds(pl.multiple_of(i * tile, tile), tile)
        grad_ref[at, :] = lax.dot_general(
            planes[at, :].astype(jnp.bfloat16), spread_ref[...], (((1,), (1,)), ((), ())),
            preferred_element_type=jnp.float32,
        ).astype(jnp.bfloat16)
        return carry

    lax.fori_loop(0, chunks, gather, 0)


def mix(projected, short_taps, li_residue, li_rate, cotangent):
    seq_len, cols = projected.shape
    chans, modes = li_rate.shape
    halves = chans // LANES
    rows = 8
    chunks = rows // halves
    source = jnp.arange(cols)[:, None]
    target = jnp.arange(cols)[None, :]
    spread = (source == 3 * (target % chans) + target // chans).astype(jnp.bfloat16)
    taps = short_taps.reshape(-1, chans, 3).transpose(0, 2, 1).reshape(-1, cols)

    def per_row(values):
        return jnp.tile(values.T.reshape(modes, halves, LANES), (1, chunks, 1))

    f32 = functools.partial(pltpu.VMEM, dtype=jnp.float32)
    vmem = pl.BlockSpec(memory_space=pltpu.VMEM)
    return pl.pallas_call(
        functools.partial(mix_kernel, seq_len, chans, modes, chunks),
        out_shape=(
            jax.ShapeDtypeStruct((chans, seq_len), jnp.bfloat16),
            jax.ShapeDtypeStruct((seq_len, cols), jnp.bfloat16),
        ),
        in_specs=[vmem] * 6,
        out_specs=(vmem, vmem),
        scratch_shapes=[
            f32((seq_len, cols)),
            f32((seq_len, cols)),
            f32((seq_len * halves, LANES)),
            f32((seq_len * halves, LANES)),
            f32((seq_len * halves, LANES)),
            f32((seq_len * halves, LANES)),
            f32((modes, rows, LANES)),
            f32((modes, rows, LANES)),
        ],
        compiler_params=pltpu.CompilerParams(vmem_limit_bytes=40 * 1024 * 1024),
        cost_estimate=pl.CostEstimate(
            flops=20 * 10**9, bytes_accessed=6 * seq_len * cols, transcendentals=0
        ),
        name="mix",
    )(projected, spread, taps, per_row(li_rate), per_row(li_residue), cotangent)


def fast_shards(tokens, w_in, short_taps, li_residue, li_rate, cotangent):
    projected = gather_multiply(tokens, w_in)
    mixed, grad = mix(projected, short_taps, li_residue, li_rate, cotangent)
    return mixed, multiply_scatter(w_in, grad)


def solution(mesh):
    n_ctx, n_tp = mesh.shape["ctx"], mesh.shape["tp"]
    body = fast_shards if (n_ctx, n_tp) == (16, 2) else shards
    in_specs = (
        P("tp", "ctx"),
        P("tp", "ctx"),
        P(None, ("ctx", "tp")),
        P(("ctx", "tp"), None),
        P(("ctx", "tp"), None),
        P(("ctx", "tp"), None),
    )
    out_specs = (P(("ctx", "tp"), None), P("ctx", "tp"))
    return jax.shard_map(body, mesh=mesh, in_specs=in_specs, out_specs=out_specs, check_vma=False)
```
